32 devices in a mesh: expert: 4 (over z), tp: 2 (over x), dp: 4 (over y, core).
Axes of the slice: x: 2, y: 2, z: 4, core: 2. Of those that a mesh axis runs over, the one named last changes fastest.
Arguments:
- hidden: bfloat16 [128, 6144], P(('expert', 'tp', 'dp')), may hold values from -400 to 400
- norm_gain: float32 [6144], replicated, may hold values from 0.1 to 1.9
- expert_ids: int32 [128, 2], P(('expert', 'tp', 'dp')), may hold values from 0 to 3, all different within a row; in each aligned block of 4 rows (0 to 3, 4 to 7, ...) at most 2 rows name the same one
- router_logits: float32 [128, 2], P(('expert', 'tp', 'dp')), may hold values from -6 to 6
- w_gate: bfloat16 [4, 6144, 8192], P('expert', None, ('tp', 'dp')), may hold values from -0.078125 to 0.078125
- w_up: bfloat16 [4, 6144, 8192], P('expert', None, ('tp', 'dp')), may hold values from -0.078125 to 0.078125
- w_down: bfloat16 [4, 8192, 6144], P('expert', ('tp', 'dp')), may hold values from -0.0625 to 0.0625
Outputs:
- moe_out: bfloat16 [128, 6144], P(('expert', 'tp', 'dp'))
The draws below stay inside these ranges and needn't reach their ends.
Inputs may be any that keep to these rules, and one draw needn't show every extreme that they name: `expert_ids`: each token names two different experts; the tokens of one device name one expert at most 2 times.
All inputs are finite; a program needn't handle non-finite values.
Results may differ from the reference program's by a relative error of at most 0.015.
Values may be sent and summed in bfloat16 or wider, within the bound.
A program may use at most 64 MiB of HBM per device.

```python
import math
import jax
import jax.numpy as jnp
import numpy as np
from jax import lax

D = 6144
FF = 8192
EXPERTS = 4
TOK_DEV = 4
MOST = 2
TOKENS = 128
N_TP = 2
N_DP = 4


def draw_hidden(key, part):
    subkeys = jax.random.split(jax.random.fold_in(key, 11), 3)
    row_scale = jnp.exp(jax.random.uniform(subkeys[0], (TOKENS, 1), jnp.float32) * math.log(10.0))
    column_scale = jnp.exp(jax.random.uniform(subkeys[1], (1, D), jnp.float32) * math.log(10.0))
    values = jnp.clip(jax.random.normal(subkeys[2], (TOKENS, D), jnp.float32), -4.0, 4.0)
    return (values * row_scale * column_scale).astype(jnp.bfloat16)


def steps_of(stream_key, dims, pieces, low, largest):
    gain, own = 1.0, jax.random.fold_in(stream_key, 6)
    for dim, blocks in pieces:
        heights = jnp.exp(jax.random.uniform(jax.random.fold_in(own, dim), (blocks,), jnp.float32, low / len(pieces), largest / len(pieces)))
        gain = gain * jnp.repeat(heights, dims[dim] // blocks).reshape([-1 if axis == dim else 1 for axis in range(len(dims))])
    return gain


def shared_out(key, own, number, rows, count, top, bound, skew):
    sequence = jax.random.permutation(key, count)
    crowded, ordinary = portions_of(count, rows * top, bound, skew, True), portions_of(count, rows * top, bound, skew, False)
    places = jnp.arange(count)

    def named(tallies, offset_by):
        used = int((tallies > 0).sum())
        fixed = max(1, used // 4)
        shifted = fixed + (places - fixed + offset_by * (used - fixed)) % max(1, count - fixed)
        return jnp.zeros((count,), jnp.int32).at[sequence[jnp.where(places < fixed, places, shifted)]].set(jnp.asarray(tallies, jnp.int32))

    tallies = jnp.where(number % 4 == 0, named(crowded, number // 4), named(ordinary, number - number // 4 - 1))
    mixed = jax.random.permutation(jax.random.fold_in(own, 3), count)
    giver, sink = mixed[0:count // 2 * 2:2], mixed[1:count // 2 * 2:2]
    slack = jnp.minimum(tallies[giver] - 1, bound - tallies[sink]) // 2
    slack = jnp.where((giver == sequence[0]) | (sink == sequence[0]) | (tallies[sink] == 0), 0, jnp.maximum(slack, 0))
    shifted = jax.random.randint(jax.random.fold_in(own, 4), (count // 2,), 0, 1 << 20) % (slack + 1)
    tallies = tallies.at[giver].add(-shifted).at[sink].add(shifted)
    labels = jnp.searchsorted(jnp.cumsum(tallies), jnp.arange(rows * top), side="right").astype(jnp.int32)
    table = labels.reshape(top, rows).T
    table = table[jax.random.permutation(jax.random.fold_in(own, 1), rows)]
    offset_by = jax.random.randint(jax.random.fold_in(own, 2), (rows, 1), 0, top)
    return jnp.take_along_axis(table, (jnp.arange(top)[None, :] + offset_by) % top, axis=1)


def portions_of(number_of, total, most, skew, full):
    loads = [(1 << 20) // math.isqrt(rank ** skew) + 1 for rank in range(1, number_of + 1)]
    largest = most if full else min(most, max(-(-total // number_of), total * loads[0] // sum(loads)))
    least = 1 if total - largest >= number_of - 1 else 0
    holding, spare = [largest] + [least] * (number_of - 1), total - largest - least * (number_of - 1)
    while spare > 0:
        candidates = [i for i in range(1, number_of) if holding[i] < largest] or [i for i in range(1, number_of) if holding[i] < most]
        mass, left = sum([loads[i] for i in candidates]), spare
        for i in candidates:
            addition = min(most - holding[i], max(1, left * loads[i] // mass), spare)
            holding[i] = holding[i] + addition
            spare = spare - addition
    return np.array(holding)


def gaussian(stream_key, extent, deviation, bound, cuts=(), kind=jnp.bfloat16):
    drawn = deviation * jax.random.normal(stream_key, extent, jnp.float32)
    if cuts:
        drawn = drawn * steps_of(stream_key, extent, cuts, -0.22, 0.18)
    return jnp.clip(drawn, -bound, bound).astype(kind)


def setup_inputs(seed: int = 0) -> dict:
    seeds = jax.random.split(jax.random.key(seed), 8)
    hidden = draw_hidden(jax.random.fold_in(seeds[7], 71), 0)
    norm_gain = jnp.clip(1.0 + 0.18 * jax.random.normal(seeds[1], (D,), jnp.float32), 0.1, 1.9)
    expert_ids_keys = jax.random.split(jax.random.fold_in(seeds[2], 1), TOKENS // TOK_DEV)
    expert_ids_turns = jax.random.permutation(jax.random.fold_in(seeds[2], 3), TOKENS // TOK_DEV)
    expert_ids = jax.vmap(lambda own, number: shared_out(jax.random.fold_in(seeds[2], 2), own, number, TOK_DEV, EXPERTS, 2, MOST, 2))(expert_ids_keys, expert_ids_turns).reshape((TOKENS, 2))
    router_logits = gaussian(seeds[3], (TOKENS, 2), 1.5, 6.0, ((0, 32),), jnp.float32)
    w_gate = gaussian(seeds[4], (EXPERTS, D, FF), D ** -0.5, 0.078125, ((0, 4), (2, 8)))
    w_up = gaussian(seeds[5], (EXPERTS, D, FF), D ** -0.5, 0.078125, ((0, 4), (2, 8)))
    w_down = gaussian(seeds[6], (EXPERTS, FF, D), FF ** -0.5, 0.0625, ((0, 4), (1, 8)))
    return dict(hidden=hidden, norm_gain=norm_gain, expert_ids=expert_ids, router_logits=router_logits, w_gate=w_gate, w_up=w_up, w_down=w_down)


def slot_table(expert_ids):
    blocks = expert_ids.shape[0] // TOK_DEV
    assigned = expert_ids.reshape(blocks, TOK_DEV * 2)
    onehot = (assigned[:, :, None] == jnp.arange(EXPERTS, dtype=jnp.int32)[None, None, :]).astype(jnp.int32)
    earlier = jnp.cumsum(onehot, axis=1) - onehot
    position = lax.optimization_barrier(jnp.sum(earlier * onehot, axis=2)).astype(jnp.int32)
    chosen = assigned[:, None, None, :] == jnp.arange(EXPERTS, dtype=jnp.int32)[None, :, None, None]
    placed = position[:, None, None, :] == jnp.arange(MOST, dtype=jnp.int32)[None, None, :, None]
    return (chosen & placed).astype(jnp.float32)

def run_expert(operands):
    expert_rows, gate_mat, up_mat, down_mat = operands
    gate_val = jnp.dot(expert_rows, gate_mat, preferred_element_type=jnp.float32)
    up_val = jnp.dot(expert_rows, up_mat, preferred_element_type=jnp.float32)
    activation = (jax.nn.silu(gate_val) * up_val).astype(jnp.bfloat16)
    shares = N_TP * N_DP
    share_width = FF // shares

    def add_share(index, total):
        start = (index * share_width).astype(jnp.int32)
        act_part = lax.dynamic_slice_in_dim(activation, start, share_width, 1)
        down_part = lax.dynamic_slice_in_dim(down_mat, start, share_width, 0)
        part = jnp.dot(act_part, down_part, preferred_element_type=jnp.float32)
        rounded = lax.optimization_barrier(part.astype(jnp.bfloat16))
        return total + rounded.astype(jnp.float32)
    total = jnp.zeros((expert_rows.shape[0], down_mat.shape[1]), jnp.float32)
    total = lax.fori_loop(jnp.int32(0), jnp.int32(shares), add_share, total)
    return total.astype(jnp.bfloat16)

def reference(hidden, norm_gain, expert_ids, router_logits, w_gate, w_up, w_down):
    values = hidden.astype(jnp.float32)
    inverse = lax.rsqrt(lax.optimization_barrier(jnp.mean(values * values, axis=1, keepdims=True)) + 1e-05)
    normed = (values * inverse * norm_gain.astype(jnp.float32)[None, :]).astype(jnp.bfloat16)
    blocks = hidden.shape[0] // TOK_DEV
    selector = slot_table(expert_ids)
    repeated = jnp.repeat(normed, 2, axis=0).reshape(blocks, TOK_DEV * 2, D).astype(jnp.float32)
    bucketed = jnp.einsum('besa,bad->ebsd', selector, repeated).astype(jnp.bfloat16)
    bucketed = bucketed.reshape(EXPERTS, blocks * MOST, D)
    produced = lax.map(run_expert, (bucketed, w_gate, w_up, w_down))
    produced = produced.reshape(EXPERTS, blocks, MOST, D).astype(jnp.float32)
    picked = jnp.einsum('besa,ebsd->bad', selector, produced).reshape(hidden.shape[0], 2, D)
    first = jax.nn.sigmoid(router_logits[:, 0] - router_logits[:, 1])
    second = jax.nn.sigmoid(router_logits[:, 1] - router_logits[:, 0])
    route_weight = jnp.stack([first, second], axis=1).astype(jnp.float32)
    combined = lax.optimization_barrier(jnp.sum(picked * route_weight[:, :, None], axis=1))
    return combined.astype(jnp.bfloat16)
```

```python
import functools

import jax
import jax.numpy as jnp
from jax import lax
from jax.experimental import pallas as pl
from jax.experimental.pallas import tpu as pltpu
from jax.sharding import PartitionSpec as P

MOST = 2
MESH = pl.DeviceIdType.MESH
F32 = jnp.float32
BF16 = jnp.bfloat16


def sigmoid(v):
    return 1.0 / (1.0 + jnp.exp(-v))


def kernel(
    experts, tps, dps, kchunks, ochunks,
    hid, gain, ids, logits, wg, wu, wd,
    out,
    wgv, wuv, wdv, zsend, zrecv, xbuf, gacc, uacc, act, psend, precv, own, rsend, rrecv, qsend, qrecv,
    wsem, dsem, zss, zrs, xss, xrs, fss, frs, pss, prs, rss, rrs, qss, qrs,
):
    tokens, width = hid.shape
    kc, oc = width // kchunks, width // ochunks
    halves = dps // 2
    group = tps * halves
    rows = experts * MOST
    me_e, me_t, me_d = lax.axis_index("expert"), lax.axis_index("tp"), lax.axis_index("dp")
    parity, half = me_d % 2, me_d // 2
    me_g = me_t * halves + half

    def z_dev(e):
        return {"expert": e, "tp": me_t, "dp": me_d}

    def g_dev(g):
        return {"expert": me_e, "tp": g // halves, "dp": (g % halves) * 2 + parity}

    partner = {"expert": me_e, "tp": me_t, "dp": half * 2 + 1 - parity}
    z_peers = [(me_e + k) % experts for k in range(1, experts)]
    g_peers = [(me_g + k) % group for k in range(1, group)]

    def remote(src, dst, ss, rs, dev):
        return pltpu.make_async_remote_copy(
            src_ref=src, dst_ref=dst, send_sem=ss, recv_sem=rs, device_id=dev, device_id_type=MESH
        )

    wcopies, dcopies = [], []
    for c in range(kchunks):
        pair = (
            pltpu.make_async_copy(wg.at[0, pl.ds(c * kc, kc), :], wgv.at[c], wsem.at[0, c]),
            pltpu.make_async_copy(wu.at[0, pl.ds(c * kc, kc), :], wuv.at[c], wsem.at[1, c]),
        )
        for copy in pair:
            copy.start()
        wcopies.append(pair)
    for j in range(ochunks):
        copy = pltpu.make_async_copy(wd.at[0, :, pl.ds(j * oc, oc)], wdv.at[j], dsem.at[j])
        copy.start()
        dcopies.append(copy)

    barrier = pltpu.get_barrier_semaphore()
    devices = [z_dev(e) for e in z_peers] + [g_dev(g) for g in g_peers] + [partner]
    for dev in devices:
        pl.semaphore_signal(barrier, inc=1, device_id=dev, device_id_type=MESH)

    values = hid[...].astype(F32)
    inverse = lax.rsqrt(jnp.mean(values * values, axis=1, keepdims=True) + 1e-05)
    normed = (values * inverse * gain[...]).astype(BF16).astype(F32)
    place = lax.broadcasted_iota(jnp.int32, (rows, 1), 0)
    expert_of, slot = place // MOST, place % MOST
    taken = jnp.zeros((rows, 1), jnp.int32)
    bucket = jnp.zeros((rows, width), F32)
    coefs = []
    for t in range(tokens):
        first = jnp.where(expert_of == ids[t, 0], 1, 0)
        names = first + jnp.where(expert_of == ids[t, 1], 1, 0)
        chosen = (names * jnp.where(taken == slot, 1, 0)).astype(F32)
        taken = taken + names
        bucket = bucket + chosen * normed[t : t + 1, :]
        gap = jnp.full((rows, 1), logits[t, 0] - logits[t, 1], F32)
        firstf = first.astype(F32)
        coefs.append(chosen * (firstf * sigmoid(gap) + (1.0 - firstf) * sigmoid(-gap)))
    for c in range(kchunks):
        for e in range(experts):
            zsend[c, e] = bucket[e * MOST : (e + 1) * MOST, c * kc : (c + 1) * kc].astype(BF16)

    pl.semaphore_wait(barrier, len(devices))

    waits = []

    def go(copy):
        copy.start()
        waits.append(copy)

    for c in range(kchunks):
        for k, e in enumerate(z_peers):
            go(remote(zsend.at[c, e], zrecv.at[c, me_e], zss.at[c, k], zrs.at[c, me_e], z_dev(e)))
    for c in range(kchunks):
        zrecv[c, me_e] = zsend[c, me_e]

    def spread(c):
        for k, e in enumerate(z_peers):
            remote(zsend.at[c, e], zrecv.at[c, e], zss.at[c, k], zrs.at[c, e], z_dev(e)).wait_recv()
        block = jnp.concatenate([zrecv[c, e].astype(F32) for e in range(experts)], axis=0)
        xbuf[c, 0, me_g] = block.astype(BF16)
        mine = xbuf.at[c, 0, me_g]
        for k, g in enumerate(g_peers):
            go(remote(mine, mine, xss.at[c, k], xrs.at[c, me_g], g_dev(g)))
        go(remote(mine, xbuf.at[c, 1, me_g], fss.at[c, 0], frs.at[c, me_g], partner))

    def forward(c):
        for k, g in enumerate(g_peers):
            here = xbuf.at[c, 0, g]
            remote(here, here, xss.at[c, k], xrs.at[c, g], g_dev(g)).wait_recv()
            go(remote(here, xbuf.at[c, 1, g], fss.at[c, k + 1], frs.at[c, g], partner))

    def enter(c):
        for g in range(group):
            there = xbuf.at[c, 1, g]
            remote(there, there, fss.at[c, 0], frs.at[c, g], partner).wait_recv()
        x = xbuf[c].astype(F32).reshape(2 * group * rows, kc).astype(BF16)
        for copy, w, acc in zip(wcopies[c], (wgv, wuv), (gacc, uacc)):
            copy.wait()
            term = jnp.dot(x, w[c], preferred_element_type=F32)
            if c == 0:
                acc[...] = term
            else:
                acc[...] += term

    for c in range(kchunks):
        spread(c)
    forward(0)
    for c in range(kchunks):
        if c + 1 < kchunks:
            forward(c + 1)
        enter(c)
    gate = gacc[...]
    act[...] = (gate * sigmoid(gate) * uacc[...]).astype(BF16)

    def down(j):
        dcopies[j].wait()
        part = jnp.dot(act[...], wdv[j], preferred_element_type=F32)
        part = part.reshape(2, group, rows, oc)
        psend[j] = part[1].astype(BF16)
        own[j] = part[0]
        go(remote(psend.at[j], precv.at[j], pss.at[j], prs.at[j], partner))

    def reduce(j):
        remote(psend.at[j], precv.at[j], pss.at[j], prs.at[j], partner).wait_recv()
        rsend[j] = (own[j] + precv[j].astype(F32)).astype(BF16)
        for k, g in enumerate(g_peers):
            go(remote(rsend.at[j, g], rrecv.at[j, me_g], rss.at[j, k], rrs.at[j, me_g], g_dev(g)))

    def home(j):
        total = rsend[j, me_g].astype(F32)
        for k, g in enumerate(g_peers):
            remote(rsend.at[j, g], rrecv.at[j, g], rss.at[j, k], rrs.at[j, g], g_dev(g)).wait_recv()
            total = total + rrecv[j, g].astype(F32)
        for e in range(experts):
            qsend[j, e] = total[e * MOST : (e + 1) * MOST, :].astype(BF16)
        for k, e in enumerate(z_peers):
            go(remote(qsend.at[j, e], qrecv.at[j, me_e], qss.at[j, k], qrs.at[j, me_e], z_dev(e)))
        qrecv[j, me_e] = qsend[j, me_e]

    def combine(j):
        for k, e in enumerate(z_peers):
            remote(qsend.at[j, e], qrecv.at[j, e], qss.at[j, k], qrs.at[j, e], z_dev(e)).wait_recv()
        back = jnp.concatenate([qrecv[j, e].astype(F32) for e in range(experts)], axis=0)
        result = [jnp.sum(back * coef, axis=0, keepdims=True) for coef in coefs]
        out[:, j * oc : (j + 1) * oc] = jnp.concatenate(result, axis=0).astype(BF16)

    stages = (down, reduce, home, combine)
    lags = (0, 1, 3, 5)
    for step in range(ochunks + lags[-1]):
        for stage, lag in zip(stages, lags):
            if 0 <= step - lag < ochunks:
                stage(step - lag)

    for copy in waits:
        copy.wait_send()


def body(hidden, norm_gain, expert_ids, router_logits, w_gate, w_up, w_down):
    experts, tps, dps = lax.axis_size("expert"), lax.axis_size("tp"), lax.axis_size("dp")
    tokens, width = hidden.shape
    inner = w_gate.shape[2]
    kchunks, ochunks = 3, 4
    kc, oc = width // kchunks, width // ochunks
    group = tps * (dps // 2)
    rows = experts * MOST
    many = 2 * group * rows
    dma = pltpu.SemaphoreType.DMA
    vmem = pl.BlockSpec(memory_space=pltpu.VMEM)
    smem = pl.BlockSpec(memory_space=pltpu.SMEM)
    hbm = pl.BlockSpec(memory_space=pl.ANY)
    return pl.pallas_call(
        functools.partial(kernel, experts, tps, dps, kchunks, ochunks),
        out_shape=jax.ShapeDtypeStruct((tokens, width), BF16),
        in_specs=[vmem, vmem, smem, smem, hbm, hbm, hbm],
        out_specs=vmem,
        scratch_shapes=[
            pltpu.VMEM((kchunks, kc, inner), BF16),
            pltpu.VMEM((kchunks, kc, inner), BF16),
            pltpu.VMEM((ochunks, inner, oc), BF16),
            pltpu.VMEM((kchunks, experts, MOST, kc), BF16),
            pltpu.VMEM((kchunks, experts, MOST, kc), BF16),
            pltpu.VMEM((kchunks, 2, group, rows, kc), BF16),
            pltpu.VMEM((many, inner), F32),
            pltpu.VMEM((many, inner), F32),
            pltpu.VMEM((many, inner), BF16),
            pltpu.VMEM((ochunks, group, rows, oc), BF16),
            pltpu.VMEM((ochunks, group, rows, oc), BF16),
            pltpu.VMEM((ochunks, group, rows, oc), F32),
            pltpu.VMEM((ochunks, group, rows, oc), BF16),
            pltpu.VMEM((ochunks, group, rows, oc), BF16),
            pltpu.VMEM((ochunks, experts, MOST, oc), BF16),
            pltpu.VMEM((ochunks, experts, MOST, oc), BF16),
            dma((2, kchunks)),
            dma((ochunks,)),
            dma((kchunks, experts)),
            dma((kchunks, experts)),
            dma((kchunks, group)),
            dma((kchunks, group)),
            dma((kchunks, group)),
            dma((kchunks, group)),
            dma((ochunks,)),
            dma((ochunks,)),
            dma((ochunks, group)),
            dma((ochunks, group)),
            dma((ochunks, experts)),
            dma((ochunks, experts)),
        ],
        compiler_params=pltpu.CompilerParams(
            collective_id=0, has_side_effects=True, vmem_limit_bytes=60 * 1024 * 1024
        ),
        cost_estimate=pl.CostEstimate(
            flops=6 * many * width * inner, bytes_accessed=6 * width * inner, transcendentals=many * inner
        ),
        name="expert_layer",
    )(hidden, norm_gain[None, :], expert_ids, router_logits, w_gate, w_up, w_down)


def solution(mesh):
    placed = (
        P(("expert", "tp", "dp"), None),
        P(),
        P(("expert", "tp", "dp"), None),
        P(("expert", "tp", "dp"), None),
        P("expert", None, ("tp", "dp")),
        P("expert", None, ("tp", "dp")),
        P("expert", ("tp", "dp"), None),
    )
    return jax.shard_map(
        body, mesh=mesh, in_specs=placed, out_specs=P(("expert", "tp", "dp"), None), check_vma=False
    )
```

```python
import functools

import jax
import jax.numpy as jnp
from jax import lax
from jax.experimental import pallas as pl
from jax.experimental.pallas import tpu as pltpu
from jax.sharding import PartitionSpec as P

MOST = 2
MESH = pl.DeviceIdType.MESH
F32 = jnp.float32
BF16 = jnp.bfloat16


def sigmoid(v):
    return 1.0 / (1.0 + jnp.exp(-v))


def kernel(
    experts, tps, dps, kchunks, ochunks,
    hid_hbm, gain_hbm, ids_hbm, logits_hbm, wg, wu, wd,
    back, coef_hbm,
    hid, gain, ids, logits, coef,
    wgv, wuv, wdv, zsend, zrecv, xbuf, gacc, uacc, act, psend, precv, own, rsend, rrecv, qsend,
    isem, wsem, dsem, zss, zrs, xss, xrs, fss, frs, pss, prs, rss, rrs, qss, qrs,
):
    tokens, width = hid_hbm.shape
    kc, oc = width // kchunks, width // ochunks
    halves = dps // 2
    group = tps * halves
    rows = experts * MOST
    me_e, me_t, me_d = lax.axis_index("expert"), lax.axis_index("tp"), lax.axis_index("dp")
    parity, half = me_d % 2, me_d // 2
    me_g = me_t * halves + half

    def z_dev(e):
        return {"expert": e, "tp": me_t, "dp": me_d}

    def g_dev(g):
        return {"expert": me_e, "tp": g // halves, "dp": (g % halves) * 2 + parity}

    partner = {"expert": me_e, "tp": me_t, "dp": half * 2 + 1 - parity}
    z_peers = [(me_e + k) % experts for k in range(1, experts)]
    g_peers = [(me_g + k) % group for k in range(1, group)]

    def remote(src, dst, ss, rs, dev):
        return pltpu.make_async_remote_copy(
            src_ref=src, dst_ref=dst, send_sem=ss, recv_sem=rs, device_id=dev, device_id_type=MESH
        )

    barrier = pltpu.get_barrier_semaphore()
    devices = [z_dev(e) for e in z_peers] + [g_dev(g) for g in g_peers] + [partner]
    for dev in devices:
        pl.semaphore_signal(barrier, inc=1, device_id=dev, device_id_type=MESH)

    small = [
        pltpu.make_async_copy(src, dst, isem.at[i])
        for i, (src, dst) in enumerate(
            [(hid_hbm, hid), (gain_hbm, gain), (ids_hbm, ids), (logits_hbm, logits)]
        )
    ]
    for copy in small:
        copy.start()

    wcopies = [
        (
            pltpu.make_async_copy(wg.at[0, pl.ds(c * kc, kc), :], wgv.at[c], wsem.at[0, c]),
            pltpu.make_async_copy(wu.at[0, pl.ds(c * kc, kc), :], wuv.at[c], wsem.at[1, c]),
        )
        for c in range(kchunks)
    ]
    dcopies = [
        pltpu.make_async_copy(wd.at[0, :, pl.ds(j * oc, oc)], wdv.at[j], dsem.at[j])
        for j in range(ochunks)
    ]

    def fetch(c):
        for copy in wcopies[c]:
            copy.start()

    fetch(0)
    for copy in small:
        copy.wait()

    values = hid[...].astype(F32)
    inverse = lax.rsqrt(jnp.mean(values * values, axis=1, keepdims=True) + 1e-05)
    normed = (values * inverse * gain[...]).astype(BF16).astype(F32)
    place = lax.broadcasted_iota(jnp.int32, (rows, 1), 0)
    expert_of, slot = place // MOST, place % MOST
    taken = jnp.zeros((rows, 1), jnp.int32)
    bucket = jnp.zeros((rows, width), F32)
    for t in range(tokens):
        first = jnp.where(expert_of == ids[0, t], 1, 0)
        names = first + jnp.where(expert_of == ids[1, t], 1, 0)
        chosen = (names * jnp.where(taken == slot, 1, 0)).astype(F32)
        taken = taken + names
        bucket = bucket + chosen * normed[t : t + 1, :]
        gap = jnp.full((rows, 1), logits[0, t] - logits[1, t], F32)
        firstf = first.astype(F32)
        coef[:, t : t + 1] = chosen * (firstf * sigmoid(gap) + (1.0 - firstf) * sigmoid(-gap))
    coef_copy = pltpu.make_async_copy(coef, coef_hbm, isem.at[4])
    coef_copy.start()
    for c in range(kchunks):
        for e in range(experts):
            zsend[c, e] = bucket[e * MOST : (e + 1) * MOST, c * kc : (c + 1) * kc].astype(BF16)

    pl.semaphore_wait(barrier, len(devices))

    waits = []

    def go(copy):
        copy.start()
        waits.append(copy)

    for c in range(kchunks):
        for k, e in enumerate(z_peers):
            go(remote(zsend.at[c, e], zrecv.at[c, me_e], zss.at[c, k], zrs.at[c, me_e], z_dev(e)))
    fetch(1)
    for c in range(kchunks):
        zrecv[c, me_e] = zsend[c, me_e]

    def spread(c):
        for k, e in enumerate(z_peers):
            remote(zsend.at[c, e], zrecv.at[c, e], zss.at[c, k], zrs.at[c, e], z_dev(e)).wait_recv()
        block = jnp.concatenate([zrecv[c, e].astype(F32) for e in range(experts)], axis=0)
        xbuf[c, 0, me_g] = block.astype(BF16)
        mine = xbuf.at[c, 0, me_g]
        for k, g in enumerate(g_peers):
            go(remote(mine, mine, xss.at[c, k], xrs.at[c, me_g], g_dev(g)))
        go(remote(mine, xbuf.at[c, 1, me_g], fss.at[c, 0], frs.at[c, me_g], partner))

    def forward(c):
        for k, g in enumerate(g_peers):
            here = xbuf.at[c, 0, g]
            remote(here, here, xss.at[c, k], xrs.at[c, g], g_dev(g)).wait_recv()
            go(remote(here, xbuf.at[c, 1, g], fss.at[c, k + 1], frs.at[c, g], partner))

    def enter(c):
        for g in range(group):
            there = xbuf.at[c, 1, g]
            remote(there, there, fss.at[c, 0], frs.at[c, g], partner).wait_recv()
        x = xbuf[c].astype(F32).reshape(2 * group * rows, kc).astype(BF16)
        for copy, w, acc in zip(wcopies[c], (wgv, wuv), (gacc, uacc)):
            copy.wait()
            term = jnp.dot(x, w[c], preferred_element_type=F32)
            if c == 0:
                acc[...] = term
            else:
                acc[...] += term

    spread(0)
    for c in range(2, kchunks):
        fetch(c)
    for c in range(1, kchunks):
        spread(c)
    dcopies[0].start()
    forward(0)
    for copy in dcopies[1:]:
        copy.start()
    for c in range(kchunks):
        if c + 1 < kchunks:
            forward(c + 1)
        enter(c)
    gate = gacc[...]
    act[...] = (gate * sigmoid(gate) * uacc[...]).astype(BF16)

    def down(j):
        dcopies[j].wait()
        part = jnp.dot(act[...], wdv[j], preferred_element_type=F32)
        part = part.reshape(2, group, rows, oc)
        psend[j] = part[1].astype(BF16)
        own[j] = part[0]
        go(remote(psend.at[j], precv.at[j], pss.at[j], prs.at[j], partner))

    def reduce(j):
        remote(psend.at[j], precv.at[j], pss.at[j], prs.at[j], partner).wait_recv()
        rsend[j] = (own[j] + precv[j].astype(F32)).astype(BF16)
        for k, g in enumerate(g_peers):
            go(remote(rsend.at[j, g], rrecv.at[j, me_g], rss.at[j, k], rrs.at[j, me_g], g_dev(g)))

    def home(j):
        total = rsend[j, me_g].astype(F32)
        for k, g in enumerate(g_peers):
            remote(rsend.at[j, g], rrecv.at[j, g], rss.at[j, k], rrs.at[j, g], g_dev(g)).wait_recv()
            total = total + rrecv[j, g].astype(F32)
        for e in range(experts):
            qsend[j, e] = total[e * MOST : (e + 1) * MOST, :].astype(BF16)
        for k, e in enumerate(z_peers):
            go(remote(qsend.at[j, e], cols(me_e, j), qss.at[j, k], qrs.at[j, me_e], z_dev(e)))
        kept.append(pltpu.make_async_copy(qsend.at[j, me_e], cols(me_e, j), qrs.at[j, me_e]))
        kept[-1].start()

    kept = []

    def cols(e, j):
        return back.at[e, :, pl.ds(j * oc, oc)]

    stages = (down, reduce, home)
    lags = (0, 1, 3)
    for step in range(ochunks + lags[-1]):
        for stage, lag in zip(stages, lags):
            if 0 <= step - lag < ochunks:
                stage(step - lag)

    for j in range(ochunks):
        for k, e in enumerate(z_peers):
            remote(qsend.at[j, e], cols(e, j), qss.at[j, k], qrs.at[j, e], z_dev(e)).wait_recv()
        kept[j].wait()
    coef_copy.wait()
    for copy in waits:
        copy.wait_send()


def body(hidden, norm_gain, expert_ids, router_logits, w_gate, w_up, w_down):
    experts, tps, dps = lax.axis_size("expert"), lax.axis_size("tp"), lax.axis_size("dp")
    tokens, width = hidden.shape
    inner = w_gate.shape[2]
    kchunks, ochunks = 3, 4
    kc, oc = width // kchunks, width // ochunks
    group = tps * (dps // 2)
    rows = experts * MOST
    many = 2 * group * rows
    dma = pltpu.SemaphoreType.DMA
    hbm = pl.BlockSpec(memory_space=pl.ANY)
    back, coef = pl.pallas_call(
        functools.partial(kernel, experts, tps, dps, kchunks, ochunks),
        out_shape=[
            jax.ShapeDtypeStruct((experts, MOST, width), BF16),
            jax.ShapeDtypeStruct((rows, tokens), F32),
        ],
        in_specs=[hbm] * 7,
        out_specs=[hbm] * 2,
        scratch_shapes=[
            pltpu.VMEM((tokens, width), BF16),
            pltpu.VMEM((1, width), F32),
            pltpu.SMEM((2, tokens), jnp.int32),
            pltpu.SMEM((2, tokens), F32),
            pltpu.VMEM((rows, tokens), F32),
            pltpu.VMEM((kchunks, kc, inner), BF16),
            pltpu.VMEM((kchunks, kc, inner), BF16),
            pltpu.VMEM((ochunks, inner, oc), BF16),
            pltpu.VMEM((kchunks, experts, MOST, kc), BF16),
            pltpu.VMEM((kchunks, experts, MOST, kc), BF16),
            pltpu.VMEM((kchunks, 2, group, rows, kc), BF16),
            pltpu.VMEM((many, inner), F32),
            pltpu.VMEM((many, inner), F32),
            pltpu.VMEM((many, inner), BF16),
            pltpu.VMEM((ochunks, group, rows, oc), BF16),
            pltpu.VMEM((ochunks, group, rows, oc), BF16),
            pltpu.VMEM((ochunks, group, rows, oc), F32),
            pltpu.VMEM((ochunks, group, rows, oc), BF16),
            pltpu.VMEM((ochunks, group, rows, oc), BF16),
            pltpu.VMEM((ochunks, experts, MOST, oc), BF16),
            dma((5,)),
            dma((2, kchunks)),
            dma((ochunks,)),
            dma((kchunks, experts)),
            dma((kchunks, experts)),
            dma((kchunks, group)),
            dma((kchunks, group)),
            dma((kchunks, group)),
            dma((kchunks, group)),
            dma((ochunks,)),
            dma((ochunks,)),
            dma((ochunks, group)),
            dma((ochunks, group)),
            dma((ochunks, experts)),
            dma((ochunks, experts)),
        ],
        compiler_params=pltpu.CompilerParams(
            collective_id=0, has_side_effects=True, vmem_limit_bytes=62 * 1024 * 1024
        ),
        cost_estimate=pl.CostEstimate(
            flops=6 * many * width * inner, bytes_accessed=6 * width * inner, transcendentals=many * inner
        ),
        name="expert_layer",
    )(hidden, norm_gain[None, :], expert_ids.T, router_logits.T, w_gate, w_up, w_down)
    weight = coef.reshape(experts, MOST, tokens)
    combined = jnp.sum(back.astype(F32)[:, :, None, :] * weight[:, :, :, None], axis=(0, 1))
    return combined.astype(BF16)


def solution(mesh):
    placed = (
        P(("expert", "tp", "dp"), None),
        P(),
        P(("expert", "tp", "dp"), None),
        P(("expert", "tp", "dp"), None),
        P("expert", None, ("tp", "dp")),
        P("expert", None, ("tp", "dp")),
        P("expert", ("tp", "dp"), None),
    )
    return jax.shard_map(
        body, mesh=mesh, in_specs=placed, out_specs=P(("expert", "tp", "dp"), None), check_vma=False
    )
```

```python
import functools

import jax
import jax.numpy as jnp
from jax import lax
from jax.experimental import pallas as pl
from jax.experimental.pallas import tpu as pltpu
from jax.sharding import PartitionSpec as P

MOST = 2
MESH = pl.DeviceIdType.MESH
F32 = jnp.float32
BF16 = jnp.bfloat16


def sigmoid(v):
    return 1.0 / (1.0 + jnp.exp(-v))


def kernel(
    experts, tps, dps, kchunks, ochunks,
    hid_hbm, gain_hbm, ids_hbm, logits_hbm, wg, wu, wd,
    back, coef_hbm,
    hid, gain, ids, logits, coef,
    wgv, wuv, wdv, zsend, zrecv, xbuf, gacc, uacc, act, psend, precv, own, rsend, rrecv, qsend,
    isem, wsem, dsem, zss, zrs, xss, xrs, fss, frs, pss, prs, rss, rrs, qss, qrs,
):
    tokens, width = hid_hbm.shape
    kc, oc = width // kchunks, width // ochunks
    halves = dps // 2
    group = tps * halves
    rows = experts * MOST
    me_e, me_t, me_d = lax.axis_index("expert"), lax.axis_index("tp"), lax.axis_index("dp")
    parity, half = me_d % 2, me_d // 2
    me_g = me_t * halves + half

    def z_dev(e):
        return {"expert": e, "tp": me_t, "dp": me_d}

    def g_dev(g):
        return {"expert": me_e, "tp": g // halves, "dp": (g % halves) * 2 + parity}

    partner = {"expert": me_e, "tp": me_t, "dp": half * 2 + 1 - parity}
    z_peers = [(me_e + k) % experts for k in range(1, experts)]
    g_peers = [(me_g + k) % group for k in range(1, group)]

    def remote(src, dst, ss, rs, dev):
        return pltpu.make_async_remote_copy(
            src_ref=src, dst_ref=dst, send_sem=ss, recv_sem=rs, device_id=dev, device_id_type=MESH
        )

    barrier = pltpu.get_barrier_semaphore()
    devices = [z_dev(e) for e in z_peers] + [g_dev(g) for g in g_peers] + [partner]
    for dev in devices:
        pl.semaphore_signal(barrier, inc=1, device_id=dev, device_id_type=MESH)

    small = [
        pltpu.make_async_copy(src, dst, isem.at[i])
        for i, (src, dst) in enumerate(
            [(hid_hbm, hid), (gain_hbm, gain), (ids_hbm, ids), (logits_hbm, logits)]
        )
    ]
    for copy in small:
        copy.start()

    wcopies = [
        (
            pltpu.make_async_copy(wg.at[0, pl.ds(c * kc, kc), :], wgv.at[c], wsem.at[0, c]),
            pltpu.make_async_copy(wu.at[0, pl.ds(c * kc, kc), :], wuv.at[c], wsem.at[1, c]),
        )
        for c in range(kchunks)
    ]
    dcopies = [
        pltpu.make_async_copy(wd.at[0, :, pl.ds(j * oc, oc)], wdv.at[j], dsem.at[j])
        for j in range(ochunks)
    ]

    def fetch(c):
        for copy in wcopies[c]:
            copy.start()

    fetch(0)
    for copy in small:
        copy.wait()

    values = hid[...].astype(F32)
    inverse = lax.rsqrt(jnp.mean(values * values, axis=1, keepdims=True) + 1e-05)
    place = lax.broadcasted_iota(jnp.int32, (rows, 1), 0)
    expert_of, slot = place // MOST, place % MOST
    taken = jnp.zeros((rows, 1), jnp.int32)
    picks, firsts = [], []
    for t in range(tokens):
        first = jnp.where(expert_of == ids[0, t], 1, 0)
        names = first + jnp.where(expert_of == ids[1, t], 1, 0)
        chosen = (names * jnp.where(taken == slot, 1, 0)).astype(F32)
        taken = taken + names
        picks.append(chosen)
        firsts.append(first.astype(F32))

    waits = []

    def go(copy):
        copy.start()
        waits.append(copy)

    def settle():
        for copy in waits:
            copy.wait_send()
        waits.clear()

    pl.semaphore_wait(barrier, len(devices))
    for c in range(kchunks):
        part = slice(c * kc, (c + 1) * kc)
        normed = (values[:, part] * inverse * gain[:, part]).astype(BF16).astype(F32)
        bucket = sum(pick * normed[t : t + 1, :] for t, pick in enumerate(picks))
        for e in range(experts):
            zsend[c, e] = bucket[e * MOST : (e + 1) * MOST, :].astype(BF16)
        for k, e in enumerate(z_peers):
            go(remote(zsend.at[c, e], zrecv.at[c, me_e], zss.at[c, k], zrs.at[c, me_e], z_dev(e)))
    fetch(1)
    for c in range(kchunks):
        zrecv[c, me_e] = zsend[c, me_e]

    def weigh():
        for t, (pick, first) in enumerate(zip(picks, firsts)):
            gap = jnp.full((rows, 1), logits[0, t] - logits[1, t], F32)
            coef[:, t : t + 1] = pick * (first * sigmoid(gap) + (1.0 - first) * sigmoid(-gap))

    coef_copy = pltpu.make_async_copy(coef, coef_hbm, isem.at[4])

    def spread(c):
        for k, e in enumerate(z_peers):
            remote(zsend.at[c, e], zrecv.at[c, e], zss.at[c, k], zrs.at[c, e], z_dev(e)).wait_recv()
        block = jnp.concatenate([zrecv[c, e].astype(F32) for e in range(experts)], axis=0)
        xbuf[c, 0, me_g] = block.astype(BF16)
        mine = xbuf.at[c, 0, me_g]
        for k, g in enumerate(g_peers):
            go(remote(mine, mine, xss.at[c, k], xrs.at[c, me_g], g_dev(g)))
        go(remote(mine, xbuf.at[c, 1, me_g], fss.at[c, 0], frs.at[c, me_g], partner))

    def forward(c):
        for k, g in enumerate(g_peers):
            here = xbuf.at[c, 0, g]
            remote(here, here, xss.at[c, k], xrs.at[c, g], g_dev(g)).wait_recv()
            go(remote(here, xbuf.at[c, 1, g], fss.at[c, k + 1], frs.at[c, g], partner))

    def enter(c):
        for g in range(group):
            there = xbuf.at[c, 1, g]
            remote(there, there, fss.at[c, 0], frs.at[c, g], partner).wait_recv()
        x = xbuf[c].astype(F32).reshape(2 * group * rows, kc).astype(BF16)
        for copy, w, acc in zip(wcopies[c], (wgv, wuv), (gacc, uacc)):
            copy.wait()
            term = jnp.dot(x, w[c], preferred_element_type=F32)
            if c == 0:
                acc[...] = term
            else:
                acc[...] += term

    spread(0)
    for c in range(2, kchunks):
        fetch(c)
    weigh()
    coef_copy.start()
    for c in range(1, kchunks):
        spread(c)
    dcopies[0].start()
    forward(0)
    for copy in dcopies[1:]:
        copy.start()
    for c in range(kchunks):
        if c + 1 < kchunks:
            forward(c + 1)
        enter(c)
    gate = gacc[...]
    act[...] = (gate * sigmoid(gate) * uacc[...]).astype(BF16)

    def down(j):
        dcopies[j].wait()
        part = jnp.dot(act[...], wdv[j], preferred_element_type=F32)
        part = part.reshape(2, group, rows, oc)
        psend[j] = part[1].astype(BF16)
        own[j] = part[0]
        go(remote(psend.at[j], precv.at[j], pss.at[j], prs.at[j], partner))

    def reduce(j):
        remote(psend.at[j], precv.at[j], pss.at[j], prs.at[j], partner).wait_recv()
        rsend[j] = (own[j] + precv[j].astype(F32)).astype(BF16)
        for k, g in enumerate(g_peers):
            go(remote(rsend.at[j, g], rrecv.at[j, me_g], rss.at[j, k], rrs.at[j, me_g], g_dev(g)))

    def home(j):
        total = rsend[j, me_g].astype(F32)
        for k, g in enumerate(g_peers):
            remote(rsend.at[j, g], rrecv.at[j, g], rss.at[j, k], rrs.at[j, g], g_dev(g)).wait_recv()
            total = total + rrecv[j, g].astype(F32)
        for e in range(experts):
            qsend[j, e] = total[e * MOST : (e + 1) * MOST, :].astype(BF16)
        for k, e in enumerate(z_peers):
            go(remote(qsend.at[j, e], cols(me_e, j), qss.at[j, k], qrs.at[j, me_e], z_dev(e)))
        kept.append(pltpu.make_async_copy(qsend.at[j, me_e], cols(me_e, j), qrs.at[j, me_e]))
        kept[-1].start()

    kept = []

    def cols(e, j):
        return back.at[e, :, pl.ds(j * oc, oc)]

    stages = (down, reduce, home)
    lags = (0, 1, 3)
    for step in range(ochunks + lags[-1]):
        if step == ochunks:
            settle()
        for stage, lag in zip(stages, lags):
            if 0 <= step - lag < ochunks:
                stage(step - lag)

    coef_copy.wait()
    settle()
    for j in range(ochunks):
        kept[j].wait()
        for k, e in enumerate(z_peers):
            remote(qsend.at[j, e], cols(e, j), qss.at[j, k], qrs.at[j, e], z_dev(e)).wait_recv()


def weighted_sum(back_hbm, coef_hbm, out, back, coef, sem):
    copies = [
        pltpu.make_async_copy(back_hbm, back, sem.at[0]),
        pltpu.make_async_copy(coef_hbm, coef, sem.at[1]),
    ]
    for copy in copies:
        copy.start()
    for copy in copies:
        copy.wait()
    experts = back.shape[0]
    rows = jnp.concatenate([back[e].astype(F32) for e in range(experts)], axis=0)
    sums = [
        jnp.sum(rows * coef[:, t : t + 1], axis=0, keepdims=True) for t in range(out.shape[0])
    ]
    out[...] = jnp.concatenate(sums, axis=0).astype(BF16)


def body(hidden, norm_gain, expert_ids, router_logits, w_gate, w_up, w_down):
    experts, tps, dps = lax.axis_size("expert"), lax.axis_size("tp"), lax.axis_size("dp")
    tokens, width = hidden.shape
    inner = w_gate.shape[2]
    kchunks, ochunks = 3, 4
    kc, oc = width // kchunks, width // ochunks
    group = tps * (dps // 2)
    rows = experts * MOST
    many = 2 * group * rows
    dma = pltpu.SemaphoreType.DMA
    hbm = pl.BlockSpec(memory_space=pl.ANY)
    back, coef = pl.pallas_call(
        functools.partial(kernel, experts, tps, dps, kchunks, ochunks),
        out_shape=[
            jax.ShapeDtypeStruct((experts, MOST, width), BF16),
            jax.ShapeDtypeStruct((rows, tokens), F32),
        ],
        in_specs=[hbm] * 7,
        out_specs=[hbm] * 2,
        scratch_shapes=[
            pltpu.VMEM((tokens, width), BF16),
            pltpu.VMEM((1, width), F32),
            pltpu.SMEM((2, tokens), jnp.int32),
            pltpu.SMEM((2, tokens), F32),
            pltpu.VMEM((rows, tokens), F32),
            pltpu.VMEM((kchunks, kc, inner), BF16),
            pltpu.VMEM((kchunks, kc, inner), BF16),
            pltpu.VMEM((ochunks, inner, oc), BF16),
            pltpu.VMEM((kchunks, experts, MOST, kc), BF16),
            pltpu.VMEM((kchunks, experts, MOST, kc), BF16),
            pltpu.VMEM((kchunks, 2, group, rows, kc), BF16),
            pltpu.VMEM((many, inner), F32),
            pltpu.VMEM((many, inner), F32),
            pltpu.VMEM((many, inner), BF16),
            pltpu.VMEM((ochunks, group, rows, oc), BF16),
            pltpu.VMEM((ochunks, group, rows, oc), BF16),
            pltpu.VMEM((ochunks, group, rows, oc), F32),
            pltpu.VMEM((ochunks, group, rows, oc), BF16),
            pltpu.VMEM((ochunks, group, rows, oc), BF16),
            pltpu.VMEM((ochunks, experts, MOST, oc), BF16),
            dma((5,)),
            dma((2, kchunks)),
            dma((ochunks,)),
            dma((kchunks, experts)),
            dma((kchunks, experts)),
            dma((kchunks, group)),
            dma((kchunks, group)),
            dma((kchunks, group)),
            dma((kchunks, group)),
            dma((ochunks,)),
            dma((ochunks,)),
            dma((ochunks, group)),
            dma((ochunks, group)),
            dma((ochunks, experts)),
            dma((ochunks, experts)),
        ],
        compiler_params=pltpu.CompilerParams(
            collective_id=0, has_side_effects=True, vmem_limit_bytes=62 * 1024 * 1024
        ),
        cost_estimate=pl.CostEstimate(
            flops=6 * many * width * inner, bytes_accessed=6 * width * inner, transcendentals=many * inner
        ),
        name="expert_layer",
    )(hidden, norm_gain[None, :], expert_ids.T, router_logits.T, w_gate, w_up, w_down)
    return pl.pallas_call(
        weighted_sum,
        out_shape=jax.ShapeDtypeStruct((tokens, width), BF16),
        in_specs=[hbm] * 2,
        out_specs=pl.BlockSpec(memory_space=pltpu.VMEM),
        scratch_shapes=[
            pltpu.VMEM(back.shape, BF16),
            pltpu.VMEM(coef.shape, F32),
            dma((2,)),
        ],
        compiler_params=pltpu.CompilerParams(vmem_limit_bytes=62 * 1024 * 1024),
        name="weighted_sum",
    )(back, coef)


def solution(mesh):
    placed = (
        P(("expert", "tp", "dp"), None),
        P(),
        P(("expert", "tp", "dp"), None),
        P(("expert", "tp", "dp"), None),
        P("expert", None, ("tp", "dp")),
        P("expert", None, ("tp", "dp")),
        P("expert", ("tp", "dp"), None),
    )
    return jax.shard_map(
        body, mesh=mesh, in_specs=placed, out_specs=P(("expert", "tp", "dp"), None), check_vma=False
    )
```

```python
import functools

import jax
import jax.numpy as jnp
from jax import lax
from jax.experimental import pallas as pl
from jax.experimental.pallas import tpu as pltpu
from jax.sharding import PartitionSpec as P

MOST = 2
MESH = pl.DeviceIdType.MESH
F32 = jnp.float32
BF16 = jnp.bfloat16


def sigmoid(v):
    return 1.0 / (1.0 + jnp.exp(-v))


def kernel(
    experts, tps, dps, kchunks, ochunks,
    hid_hbm, gain_hbm, ids_hbm, logits_hbm, wg, wu, wd,
    back, coef_hbm,
    hid, gain, ids, logits, coef,
    wgv, wuv, wdv, zsend, zrecv, xbuf, gacc, uacc, act, psend, precv, own, rsend, rrecv, qsend,
    isem, wsem, dsem, zss, zrs, xss, xrs, fss, frs, pss, prs, rss, rrs, qss, qrs,
):
    tokens, width = hid_hbm.shape
    kc, oc = width // kchunks, width // ochunks
    halves = dps // 2
    group = tps * halves
    rows = experts * MOST
    me_e, me_t, me_d = lax.axis_index("expert"), lax.axis_index("tp"), lax.axis_index("dp")
    parity, half = me_d % 2, me_d // 2
    me_g = me_t * halves + half

    def z_dev(e):
        return {"expert": e, "tp": me_t, "dp": me_d}

    def g_dev(g):
        return {"expert": me_e, "tp": g // halves, "dp": (g % halves) * 2 + parity}

    partner = {"expert": me_e, "tp": me_t, "dp": half * 2 + 1 - parity}
    z_peers = [(me_e + k) % experts for k in range(1, experts)]
    g_peers = [(me_g + k) % group for k in range(1, group)]

    def remote(src, dst, ss, rs, dev):
        return pltpu.make_async_remote_copy(
            src_ref=src, dst_ref=dst, send_sem=ss, recv_sem=rs, device_id=dev, device_id_type=MESH
        )

    barrier = pltpu.get_barrier_semaphore()
    devices = [z_dev(e) for e in z_peers] + [g_dev(g) for g in g_peers] + [partner]
    for dev in devices:
        pl.semaphore_signal(barrier, inc=1, device_id=dev, device_id_type=MESH)

    small = [
        pltpu.make_async_copy(src, dst, isem.at[i])
        for i, (src, dst) in enumerate(
            [(hid_hbm, hid), (gain_hbm, gain), (ids_hbm, ids), (logits_hbm, logits)]
        )
    ]
    for copy in small:
        copy.start()

    wcopies = [
        (
            pltpu.make_async_copy(wg.at[0, pl.ds(c * kc, kc), :], wgv.at[c], wsem.at[0, c]),
            pltpu.make_async_copy(wu.at[0, pl.ds(c * kc, kc), :], wuv.at[c], wsem.at[1, c]),
        )
        for c in range(kchunks)
    ]
    dcopies = [
        pltpu.make_async_copy(wd.at[0, :, pl.ds(j * oc, oc)], wdv.at[j], dsem.at[j])
        for j in range(ochunks)
    ]

    def fetch(c):
        for copy in wcopies[c]:
            copy.start()

    for c in range(kchunks):
        fetch(c)
    for copy in dcopies:
        copy.start()
    for copy in small:
        copy.wait()

    values = hid[...].astype(F32)
    inverse = lax.rsqrt(jnp.mean(values * values, axis=1, keepdims=True) + 1e-05)
    place = lax.broadcasted_iota(jnp.int32, (rows, 1), 0)
    expert_of, slot = place // MOST, place % MOST
    taken = jnp.zeros((rows, 1), jnp.int32)
    picks, firsts = [], []
    for t in range(tokens):
        first = jnp.where(expert_of == ids[0, t], 1, 0)
        names = first + jnp.where(expert_of == ids[1, t], 1, 0)
        chosen = (names * jnp.where(taken == slot, 1, 0)).astype(F32)
        taken = taken + names
        picks.append(chosen)
        firsts.append(first.astype(F32))

    waits = []

    def go(copy):
        copy.start()
        waits.append(copy)

    def settle():
        for copy in waits:
            copy.wait_send()
        waits.clear()

    for c in range(kchunks):
        part = slice(c * kc, (c + 1) * kc)
        normed = (values[:, part] * inverse * gain[:, part]).astype(BF16).astype(F32)
        bucket = sum(pick * normed[t : t + 1, :] for t, pick in enumerate(picks))
        for e in range(experts):
            zsend[c, e] = bucket[e * MOST : (e + 1) * MOST, :].astype(BF16)
    pl.semaphore_wait(barrier, len(devices))
    for c in range(kchunks):
        for k, e in enumerate(z_peers):
            go(remote(zsend.at[c, e], zrecv.at[c, me_e], zss.at[c, k], zrs.at[c, me_e], z_dev(e)))
    for c in range(kchunks):
        zrecv[c, me_e] = zsend[c, me_e]

    def weigh():
        for t, (pick, first) in enumerate(zip(picks, firsts)):
            gap = jnp.full((rows, 1), logits[0, t] - logits[1, t], F32)
            coef[:, t : t + 1] = pick * (first * sigmoid(gap) + (1.0 - first) * sigmoid(-gap))

    coef_copy = pltpu.make_async_copy(coef, coef_hbm, isem.at[4])

    def spread(c):
        for k, e in enumerate(z_peers):
            remote(zsend.at[c, e], zrecv.at[c, e], zss.at[c, k], zrs.at[c, e], z_dev(e)).wait_recv()
        block = jnp.concatenate([zrecv[c, e].astype(F32) for e in range(experts)], axis=0)
        xbuf[c, 0, me_g] = block.astype(BF16)
        mine = xbuf.at[c, 0, me_g]
        for k, g in enumerate(g_peers):
            go(remote(mine, mine, xss.at[c, k], xrs.at[c, me_g], g_dev(g)))
        go(remote(mine, xbuf.at[c, 1, me_g], fss.at[c, 0], frs.at[c, me_g], partner))

    def forward(c):
        for k, g in enumerate(g_peers):
            here = xbuf.at[c, 0, g]
            remote(here, here, xss.at[c, k], xrs.at[c, g], g_dev(g)).wait_recv()
            go(remote(here, xbuf.at[c, 1, g], fss.at[c, k + 1], frs.at[c, g], partner))

    def enter(c):
        for g in range(group):
            there = xbuf.at[c, 1, g]
            remote(there, there, fss.at[c, 0], frs.at[c, g], partner).wait_recv()
        x = xbuf[c].astype(F32).reshape(2 * group * rows, kc).astype(BF16)
        for copy, w, acc in zip(wcopies[c], (wgv, wuv), (gacc, uacc)):
            copy.wait()
            term = jnp.dot(x, w[c], preferred_element_type=F32)
            if c == 0:
                acc[...] = term
            else:
                acc[...] += term

    for c in range(kchunks):
        spread(c)
    forward(0)
    for c in range(kchunks):
        if c + 1 < kchunks:
            forward(c + 1)
        enter(c)
    gate = gacc[...]
    act[...] = (gate * sigmoid(gate) * uacc[...]).astype(BF16)

    def down(j):
        dcopies[j].wait()
        part = jnp.dot(act[...], wdv[j], preferred_element_type=F32)
        part = part.reshape(2, group, rows, oc)
        psend[j] = part[1].astype(BF16)
        own[j] = part[0]
        go(remote(psend.at[j], precv.at[j], pss.at[j], prs.at[j], partner))

    def reduce(j):
        remote(psend.at[j], precv.at[j], pss.at[j], prs.at[j], partner).wait_recv()
        rsend[j] = (own[j] + precv[j].astype(F32)).astype(BF16)
        for k, g in enumerate(g_peers):
            go(remote(rsend.at[j, g], rrecv.at[j, me_g], rss.at[j, k], rrs.at[j, me_g], g_dev(g)))

    def home(j):
        total = rsend[j, me_g].astype(F32)
        for k, g in enumerate(g_peers):
            remote(rsend.at[j, g], rrecv.at[j, g], rss.at[j, k], rrs.at[j, g], g_dev(g)).wait_recv()
            total = total + rrecv[j, g].astype(F32)
        for e in range(experts):
            qsend[j, e] = total[e * MOST : (e + 1) * MOST, :].astype(BF16)
        for k, e in enumerate(z_peers):
            go(remote(qsend.at[j, e], cols(me_e, j), qss.at[j, k], qrs.at[j, me_e], z_dev(e)))
        kept.append(pltpu.make_async_copy(qsend.at[j, me_e], cols(me_e, j), qrs.at[j, me_e]))
        kept[-1].start()

    kept = []

    def cols(e, j):
        return back.at[e, :, pl.ds(j * oc, oc)]

    stages = (down, reduce, home)
    lags = (0, 1, 3)
    for step in range(ochunks + lags[-1]):
        for stage, lag in zip(stages, lags):
            if 0 <= step - lag < ochunks:
                stage(step - lag)

    weigh()
    coef_copy.start()
    settle()
    coef_copy.wait()
    for j in range(ochunks):
        kept[j].wait()
        for k, e in enumerate(z_peers):
            remote(qsend.at[j, e], cols(e, j), qss.at[j, k], qrs.at[j, e], z_dev(e)).wait_recv()


def weighted_sum(back_hbm, coef_hbm, out, back, coef, sem):
    copies = [
        pltpu.make_async_copy(back_hbm, back, sem.at[0]),
        pltpu.make_async_copy(coef_hbm, coef, sem.at[1]),
    ]
    for copy in copies:
        copy.start()
    for copy in copies:
        copy.wait()
    experts = back.shape[0]
    rows = jnp.concatenate([back[e].astype(F32) for e in range(experts)], axis=0)
    sums = [
        jnp.sum(rows * coef[:, t : t + 1], axis=0, keepdims=True) for t in range(out.shape[0])
    ]
    out[...] = jnp.concatenate(sums, axis=0).astype(BF16)


def body(hidden, norm_gain, expert_ids, router_logits, w_gate, w_up, w_down):
    experts, tps, dps = lax.axis_size("expert"), lax.axis_size("tp"), lax.axis_size("dp")
    tokens, width = hidden.shape
    inner = w_gate.shape[2]
    kchunks, ochunks = 3, 6
    kc, oc = width // kchunks, width // ochunks
    group = tps * (dps // 2)
    rows = experts * MOST
    many = 2 * group * rows
    dma = pltpu.SemaphoreType.DMA
    hbm = pl.BlockSpec(memory_space=pl.ANY)
    back, coef = pl.pallas_call(
        functools.partial(kernel, experts, tps, dps, kchunks, ochunks),
        out_shape=[
            jax.ShapeDtypeStruct((experts, MOST, width), BF16),
            jax.ShapeDtypeStruct((rows, tokens), F32),
        ],
        in_specs=[hbm] * 7,
        out_specs=[hbm] * 2,
        scratch_shapes=[
            pltpu.VMEM((tokens, width), BF16),
            pltpu.VMEM((1, width), F32),
            pltpu.SMEM((2, tokens), jnp.int32),
            pltpu.SMEM((2, tokens), F32),
            pltpu.VMEM((rows, tokens), F32),
            pltpu.VMEM((kchunks, kc, inner), BF16),
            pltpu.VMEM((kchunks, kc, inner), BF16),
            pltpu.VMEM((ochunks, inner, oc), BF16),
            pltpu.VMEM((kchunks, experts, MOST, kc), BF16),
            pltpu.VMEM((kchunks, experts, MOST, kc), BF16),
            pltpu.VMEM((kchunks, 2, group, rows, kc), BF16),
            pltpu.VMEM((many, inner), F32),
            pltpu.VMEM((many, inner), F32),
            pltpu.VMEM((many, inner), BF16),
            pltpu.VMEM((ochunks, group, rows, oc), BF16),
            pltpu.VMEM((ochunks, group, rows, oc), BF16),
            pltpu.VMEM((ochunks, group, rows, oc), F32),
            pltpu.VMEM((ochunks, group, rows, oc), BF16),
            pltpu.VMEM((ochunks, group, rows, oc), BF16),
            pltpu.VMEM((ochunks, experts, MOST, oc), BF16),
            dma((5,)),
            dma((2, kchunks)),
            dma((ochunks,)),
            dma((kchunks, experts)),
            dma((kchunks, experts)),
            dma((kchunks, group)),
            dma((kchunks, group)),
            dma((kchunks, group)),
            dma((kchunks, group)),
            dma((ochunks,)),
            dma((ochunks,)),
            dma((ochunks, group)),
            dma((ochunks, group)),
            dma((ochunks, experts)),
            dma((ochunks, experts)),
        ],
        compiler_params=pltpu.CompilerParams(
            collective_id=0, has_side_effects=True, vmem_limit_bytes=62 * 1024 * 1024
        ),
        cost_estimate=pl.CostEstimate(
            flops=6 * many * width * inner, bytes_accessed=6 * width * inner, transcendentals=many * inner
        ),
        name="expert_layer",
    )(hidden, norm_gain[None, :], expert_ids.T, router_logits.T, w_gate, w_up, w_down)
    return pl.pallas_call(
        weighted_sum,
        out_shape=jax.ShapeDtypeStruct((tokens, width), BF16),
        in_specs=[hbm] * 2,
        out_specs=pl.BlockSpec(memory_space=pltpu.VMEM),
        scratch_shapes=[
            pltpu.VMEM(back.shape, BF16),
            pltpu.VMEM(coef.shape, F32),
            dma((2,)),
        ],
        compiler_params=pltpu.CompilerParams(vmem_limit_bytes=62 * 1024 * 1024),
        name="weighted_sum",
    )(back, coef)


def solution(mesh):
    placed = (
        P(("expert", "tp", "dp"), None),
        P(),
        P(("expert", "tp", "dp"), None),
        P(("expert", "tp", "dp"), None),
        P("expert", None, ("tp", "dp")),
        P("expert", None, ("tp", "dp")),
        P("expert", ("tp", "dp"), None),
    )
    return jax.shard_map(
        body, mesh=mesh, in_specs=placed, out_specs=P(("expert", "tp", "dp"), None), check_vma=False
    )
```

```python
import functools

import jax
import jax.numpy as jnp
from jax import lax
from jax.experimental import pallas as pl
from jax.experimental.pallas import tpu as pltpu
from jax.sharding import PartitionSpec as P

MOST = 2
MESH = pl.DeviceIdType.MESH
F32 = jnp.float32
BF16 = jnp.bfloat16


def sigmoid(v):
    return 1.0 / (1.0 + jnp.exp(-v))


def kernel(
    experts, tps, dps, kchunks, ochunks,
    hid_hbm, gain_hbm, ids_hbm, logits_hbm, wg, wu, wd,
    back, coef_hbm,
    hid, gain, ids, logits, coef,
    wgv, wuv, wdv, zsend, zrecv, xbuf, gacc, uacc, act, psend, precv, own, rsend, rrecv, qsend,
    isem, wsem, dsem, zss, zrs, xss, xrs, fss, frs, pss, prs, rss, rrs, qss, qrs,
):
    tokens, width = hid_hbm.shape
    kc, oc = width // kchunks, width // ochunks
    halves = dps // 2
    group = tps * halves
    rows = experts * MOST
    me_e, me_t, me_d = lax.axis_index("expert"), lax.axis_index("tp"), lax.axis_index("dp")
    parity, half = me_d % 2, me_d // 2
    me_g = me_t * halves + half

    def z_dev(e):
        return {"expert": e, "tp": me_t, "dp": me_d}

    def g_dev(g):
        return {"expert": me_e, "tp": g // halves, "dp": (g % halves) * 2 + parity}

    partner = {"expert": me_e, "tp": me_t, "dp": half * 2 + 1 - parity}
    z_peers = [(me_e + k) % experts for k in range(1, experts)]
    g_peers = [(me_g + k) % group for k in range(1, group)]

    def remote(src, dst, ss, rs, dev):
        return pltpu.make_async_remote_copy(
            src_ref=src, dst_ref=dst, send_sem=ss, recv_sem=rs, device_id=dev, device_id_type=MESH
        )

    barrier = pltpu.get_barrier_semaphore()
    devices = [z_dev(e) for e in z_peers] + [g_dev(g) for g in g_peers] + [partner]
    for dev in devices:
        pl.semaphore_signal(barrier, inc=1, device_id=dev, device_id_type=MESH)

    small = [
        pltpu.make_async_copy(src, dst, isem.at[i])
        for i, (src, dst) in enumerate(
            [(hid_hbm, hid), (gain_hbm, gain), (ids_hbm, ids), (logits_hbm, logits)]
        )
    ]
    for copy in small:
        copy.start()

    wcopies = [
        (
            pltpu.make_async_copy(wg.at[0, pl.ds(c * kc, kc), :], wgv.at[c], wsem.at[0, c]),
            pltpu.make_async_copy(wu.at[0, pl.ds(c * kc, kc), :], wuv.at[c], wsem.at[1, c]),
        )
        for c in range(kchunks)
    ]
    dcopies = [
        pltpu.make_async_copy(wd.at[0, :, pl.ds(j * oc, oc)], wdv.at[j], dsem.at[j])
        for j in range(ochunks)
    ]

    def fetch(c):
        for copy in wcopies[c]:
            copy.start()

    fetch(0)
    for copy in small:
        copy.wait()

    values = hid[...].astype(F32)
    inverse = lax.rsqrt(jnp.mean(values * values, axis=1, keepdims=True) + 1e-05)
    place = lax.broadcasted_iota(jnp.int32, (rows, 1), 0)
    expert_of, slot = place // MOST, place % MOST
    taken = jnp.zeros((rows, 1), jnp.int32)
    picks, firsts = [], []
    for t in range(tokens):
        first = jnp.where(expert_of == ids[0, t], 1, 0)
        names = first + jnp.where(expert_of == ids[1, t], 1, 0)
        chosen = (names * jnp.where(taken == slot, 1, 0)).astype(F32)
        taken = taken + names
        picks.append(chosen)
        firsts.append(first.astype(F32))

    waits = []

    def go(copy):
        copy.start()
        waits.append(copy)

    def settle():
        for copy in waits:
            copy.wait_send()
        waits.clear()

    for c in range(kchunks):
        part = slice(c * kc, (c + 1) * kc)
        normed = (values[:, part] * inverse * gain[:, part]).astype(BF16).astype(F32)
        bucket = sum(pick * normed[t : t + 1, :] for t, pick in enumerate(picks))
        for e in range(experts):
            zsend[c, e] = bucket[e * MOST : (e + 1) * MOST, :].astype(BF16)
    pl.semaphore_wait(barrier, len(devices))
    for c in range(kchunks):
        for k, e in enumerate(z_peers):
            go(remote(zsend.at[c, e], zrecv.at[c, me_e], zss.at[c, k], zrs.at[c, me_e], z_dev(e)))
    for c in range(1, kchunks):
        fetch(c)
    for c in range(kchunks):
        zrecv[c, me_e] = zsend[c, me_e]

    def weigh():
        for t, (pick, first) in enumerate(zip(picks, firsts)):
            gap = jnp.full((rows, 1), logits[0, t] - logits[1, t], F32)
            coef[:, t : t + 1] = pick * (first * sigmoid(gap) + (1.0 - first) * sigmoid(-gap))

    coef_copy = pltpu.make_async_copy(coef, coef_hbm, isem.at[4])

    def spread(c):
        for k, e in enumerate(z_peers):
            remote(zsend.at[c, e], zrecv.at[c, e], zss.at[c, k], zrs.at[c, e], z_dev(e)).wait_recv()
        block = jnp.concatenate([zrecv[c, e].astype(F32) for e in range(experts)], axis=0)
        xbuf[c, 0, me_g] = block.astype(BF16)
        mine = xbuf.at[c, 0, me_g]
        for k, g in enumerate(g_peers):
            go(remote(mine, mine, xss.at[c, k], xrs.at[c, me_g], g_dev(g)))
        go(remote(mine, xbuf.at[c, 1, me_g], fss.at[c, 0], frs.at[c, me_g], partner))

    def forward(c):
        for k, g in enumerate(g_peers):
            here = xbuf.at[c, 0, g]
            remote(here, here, xss.at[c, k], xrs.at[c, g], g_dev(g)).wait_recv()
            go(remote(here, xbuf.at[c, 1, g], fss.at[c, k + 1], frs.at[c, g], partner))

    def enter(c):
        for g in range(group):
            there = xbuf.at[c, 1, g]
            remote(there, there, fss.at[c, 0], frs.at[c, g], partner).wait_recv()
        x = xbuf[c].astype(F32).reshape(2 * group * rows, kc).astype(BF16)
        for copy, w, acc in zip(wcopies[c], (wgv, wuv), (gacc, uacc)):
            copy.wait()
            term = jnp.dot(x, w[c], preferred_element_type=F32)
            if c == 0:
                acc[...] = term
            else:
                acc[...] += term

    for c in range(kchunks):
        spread(c)
    dcopies[0].start()
    forward(0)
    for copy in dcopies[1:]:
        copy.start()
    for c in range(kchunks):
        if c + 1 < kchunks:
            forward(c + 1)
        enter(c)
    gate = gacc[...]
    act[...] = (gate * sigmoid(gate) * uacc[...]).astype(BF16)

    def down(j):
        dcopies[j].wait()
        part = jnp.dot(act[...], wdv[j], preferred_element_type=F32)
        part = part.reshape(2, group, rows, oc)
        psend[j] = part[1].astype(BF16)
        own[j] = part[0]
        go(remote(psend.at[j], precv.at[j], pss.at[j], prs.at[j], partner))

    def reduce(j):
        remote(psend.at[j], precv.at[j], pss.at[j], prs.at[j], partner).wait_recv()
        rsend[j] = (own[j] + precv[j].astype(F32)).astype(BF16)
        for k, g in enumerate(g_peers):
            go(remote(rsend.at[j, g], rrecv.at[j, me_g], rss.at[j, k], rrs.at[j, me_g], g_dev(g)))

    def home(j):
        total = rsend[j, me_g].astype(F32)
        for k, g in enumerate(g_peers):
            remote(rsend.at[j, g], rrecv.at[j, g], rss.at[j, k], rrs.at[j, g], g_dev(g)).wait_recv()
            total = total + rrecv[j, g].astype(F32)
        for e in range(experts):
            qsend[j, e] = total[e * MOST : (e + 1) * MOST, :].astype(BF16)
        for k, e in enumerate(z_peers):
            go(remote(qsend.at[j, e], cols(me_e, j), qss.at[j, k], qrs.at[j, me_e], z_dev(e)))
        kept.append(pltpu.make_async_copy(qsend.at[j, me_e], cols(me_e, j), qrs.at[j, me_e]))
        kept[-1].start()

    kept = []

    def cols(e, j):
        return back.at[e, :, pl.ds(j * oc, oc)]

    stages = (down, reduce, home)
    lags = (0, 1, 3)
    for step in range(ochunks + lags[-1]):
        for stage, lag in zip(stages, lags):
            if 0 <= step - lag < ochunks:
                stage(step - lag)

    weigh()
    coef_copy.start()
    settle()
    coef_copy.wait()
    for j in range(ochunks):
        kept[j].wait()
        for k, e in enumerate(z_peers):
            remote(qsend.at[j, e], cols(e, j), qss.at[j, k], qrs.at[j, e], z_dev(e)).wait_recv()


def weighted_sum(back_hbm, coef_hbm, out, back, coef, sem):
    copies = [
        pltpu.make_async_copy(back_hbm, back, sem.at[0]),
        pltpu.make_async_copy(coef_hbm, coef, sem.at[1]),
    ]
    for copy in copies:
        copy.start()
    for copy in copies:
        copy.wait()
    experts = back.shape[0]
    rows = jnp.concatenate([back[e].astype(F32) for e in range(experts)], axis=0)
    sums = [
        jnp.sum(rows * coef[:, t : t + 1], axis=0, keepdims=True) for t in range(out.shape[0])
    ]
    out[...] = jnp.concatenate(sums, axis=0).astype(BF16)


def body(hidden, norm_gain, expert_ids, router_logits, w_gate, w_up, w_down):
    experts, tps, dps = lax.axis_size("expert"), lax.axis_size("tp"), lax.axis_size("dp")
    tokens, width = hidden.shape
    inner = w_gate.shape[2]
    kchunks, ochunks = 2, 3
    kc, oc = width // kchunks, width // ochunks
    group = tps * (dps // 2)
    rows = experts * MOST
    many = 2 * group * rows
    dma = pltpu.SemaphoreType.DMA
    hbm = pl.BlockSpec(memory_space=pl.ANY)
    back, coef = pl.pallas_call(
        functools.partial(kernel, experts, tps, dps, kchunks, ochunks),
        out_shape=[
            jax.ShapeDtypeStruct((experts, MOST, width), BF16),
            jax.ShapeDtypeStruct((rows, tokens), F32),
        ],
        in_specs=[hbm] * 7,
        out_specs=[hbm] * 2,
        scratch_shapes=[
            pltpu.VMEM((tokens, width), BF16),
            pltpu.VMEM((1, width), F32),
            pltpu.SMEM((2, tokens), jnp.int32),
            pltpu.SMEM((2, tokens), F32),
            pltpu.VMEM((rows, tokens), F32),
            pltpu.VMEM((kchunks, kc, inner), BF16),
            pltpu.VMEM((kchunks, kc, inner), BF16),
            pltpu.VMEM((ochunks, inner, oc), BF16),
            pltpu.VMEM((kchunks, experts, MOST, kc), BF16),
            pltpu.VMEM((kchunks, experts, MOST, kc), BF16),
            pltpu.VMEM((kchunks, 2, group, rows, kc), BF16),
            pltpu.VMEM((many, inner), F32),
            pltpu.VMEM((many, inner), F32),
            pltpu.VMEM((many, inner), BF16),
            pltpu.VMEM((ochunks, group, rows, oc), BF16),
            pltpu.VMEM((ochunks, group, rows, oc), BF16),
            pltpu.VMEM((ochunks, group, rows, oc), F32),
            pltpu.VMEM((ochunks, group, rows, oc), BF16),
            pltpu.VMEM((ochunks, group, rows, oc), BF16),
            pltpu.VMEM((ochunks, experts, MOST, oc), BF16),
            dma((5,)),
            dma((2, kchunks)),
            dma((ochunks,)),
            dma((kchunks, experts)),
            dma((kchunks, experts)),
            dma((kchunks, group)),
            dma((kchunks, group)),
            dma((kchunks, group)),
            dma((kchunks, group)),
            dma((ochunks,)),
            dma((ochunks,)),
            dma((ochunks, group)),
            dma((ochunks, group)),
            dma((ochunks, experts)),
            dma((ochunks, experts)),
        ],
        compiler_params=pltpu.CompilerParams(
            collective_id=0, has_side_effects=True, vmem_limit_bytes=62 * 1024 * 1024
        ),
        cost_estimate=pl.CostEstimate(
            flops=6 * many * width * inner, bytes_accessed=6 * width * inner, transcendentals=many * inner
        ),
        name="expert_layer",
    )(hidden, norm_gain[None, :], expert_ids.T, router_logits.T, w_gate, w_up, w_down)
    return pl.pallas_call(
        weighted_sum,
        out_shape=jax.ShapeDtypeStruct((tokens, width), BF16),
        in_specs=[hbm] * 2,
        out_specs=pl.BlockSpec(memory_space=pltpu.VMEM),
        scratch_shapes=[
            pltpu.VMEM(back.shape, BF16),
            pltpu.VMEM(coef.shape, F32),
            dma((2,)),
        ],
        compiler_params=pltpu.CompilerParams(vmem_limit_bytes=62 * 1024 * 1024),
        name="weighted_sum",
    )(back, coef)


def solution(mesh):
    placed = (
        P(("expert", "tp", "dp"), None),
        P(),
        P(("expert", "tp", "dp"), None),
        P(("expert", "tp", "dp"), None),
        P("expert", None, ("tp", "dp")),
        P("expert", None, ("tp", "dp")),
        P("expert", ("tp", "dp"), None),
    )
    return jax.shard_map(
        body, mesh=mesh, in_specs=placed, out_specs=P(("expert", "tp", "dp"), None), check_vma=False
    )
```
